32 devices in a mesh: chan: 4 (over z), row: 4 (over x, core), col: 2 (over y).
Axes of the slice: x: 2, y: 2, z: 4, core: 2. Of those that a mesh axis runs over, the one named last changes fastest.
Arguments:
- voltages: bfloat16 [4, 4096, 512], P(None, ('chan', 'row', 'col')), may hold values from -6 to 6
- anchor_u_cells: int32 [4, 1024, 1024], P('chan', 'row', 'col'), may hold values from 0 to 255
- anchor_v_cells: int32 [4, 1024, 1024], P('chan', 'row', 'col'), may hold values from 0 to 255
- tile_kernel_offsets: int32 [4, 1024, 1024], P('chan', 'row', 'col'), may hold values from 0 to 63
- kernel_u: float32 [8, 32], replicated, may hold values from -3 to 3
- kernel_v: float32 [8, 32], replicated, may hold values from -3 to 3
Outputs:
- uv_grid: float32 [4, 2, 256, 256], P('chan', None, ('row', 'col'))
The draws below stay inside these ranges and needn't reach their ends.
Inputs may be any that keep to these rules, and one draw needn't show every extreme that they name: tile_kernel_offsets holds ku * 8 + kv.
All inputs are finite; a program needn't handle non-finite values.
Results may differ from the reference program's by a relative error of at most 0.0029.
Values may be sent and summed in bfloat16 or wider, within the bound.
A program may use at most 512 MiB of HBM per device.

```python
import jax
import jax.numpy as jnp
from jax import lax

INPUT_COUNT = 4096
SAMPLE_COUNT = 256
TILE_SIDE = 4
PATCH = 8
KERNEL_STEPS = 8
GRID_SIDE = 256
CHANNEL_TOTAL = 4


def with_ends(values, stream_key, smallest, high):
    place = [jax.random.randint(jax.random.fold_in(stream_key, axis), (), 0, length) for axis, length in enumerate(values.shape)]
    main_axis = values.shape.index(max(values.shape))
    beside = place[:main_axis] + [(place[main_axis] + 1) % values.shape[main_axis]] + place[main_axis + 1:]
    return values.at[tuple(place)].set(smallest).at[tuple(beside)].set(high)


def shard_levels(key, extent, cuts, smallest, largest):
    def one(position, blocks):
        draws = jax.random.uniform(jax.random.fold_in(jax.random.fold_in(key, 6), position), (blocks,), jnp.float32, smallest / len(cuts), largest / len(cuts))
        return jnp.repeat(jnp.exp(draws), extent[position] // blocks).reshape((-1,) + (1,) * (len(extent) - position - 1))

    loudness = one(*cuts[0])
    for cut in cuts[1:]:
        loudness = loudness * one(*cut)
    return loudness


def normal_values(key, shape, width, bound, split=(), kind=jnp.bfloat16):
    result = width * jax.random.normal(key, shape, jnp.float32)
    if split:
        result = result * shard_levels(key, shape, split, -0.22, 0.18)
    return jnp.clip(result, -bound, bound).astype(kind)


def setup_inputs(seed: int = 0) -> dict:
    key_list = jax.random.split(jax.random.key(seed), 7)
    return {
        "voltages": normal_values(key_list[0], (CHANNEL_TOTAL, INPUT_COUNT, 2 * SAMPLE_COUNT), 1.0, 6.0, ((1, 32),)),
        "anchor_u_cells": with_ends(jax.random.randint(key_list[1], (CHANNEL_TOTAL, INPUT_COUNT // TILE_SIDE, INPUT_COUNT // TILE_SIDE), 0, GRID_SIDE), jax.random.fold_in(key_list[1], 1), 0, GRID_SIDE - 1).astype(jnp.int32),
        "anchor_v_cells": with_ends(jax.random.randint(key_list[2], (CHANNEL_TOTAL, INPUT_COUNT // TILE_SIDE, INPUT_COUNT // TILE_SIDE), 0, GRID_SIDE), jax.random.fold_in(key_list[2], 1), 0, GRID_SIDE - 1).astype(jnp.int32),
        "tile_kernel_offsets": with_ends(jax.random.randint(key_list[3], (CHANNEL_TOTAL, INPUT_COUNT // TILE_SIDE, INPUT_COUNT // TILE_SIDE), 0, KERNEL_STEPS * KERNEL_STEPS), jax.random.fold_in(key_list[3], 1), 0, (KERNEL_STEPS * KERNEL_STEPS) - 1).astype(jnp.int32),
        "kernel_u": normal_values(key_list[4], (KERNEL_STEPS, PATCH * TILE_SIDE), 0.35, 3.0, (), jnp.float32),
        "kernel_v": normal_values(key_list[5], (KERNEL_STEPS, PATCH * TILE_SIDE), 0.35, 3.0, (), jnp.float32),
    }


def tile_patches(vis_block, kern_left, kern_right):
    partial_sums = vis_block[:, :, 0, None, :] * kern_right[None, None, :, 0, :]
    for index_l in range(1, TILE_SIDE):
        partial_sums = partial_sums + vis_block[:, :, index_l, None, :] * kern_right[None, None, :, index_l, :]
    shaped = kern_left[None, :, 0, None, :] * partial_sums[:, None, 0, :, :]
    for index_k in range(1, TILE_SIDE):
        shaped = shaped + kern_left[None, :, index_k, None, :] * partial_sums[:, None, index_k, :, :]
    return shaped.reshape(2 * PATCH * PATCH, shaped.shape[-1])


def fold_grid(patched):
    pieces = patched.reshape(2, PATCH, PATCH, GRID_SIDE, GRID_SIDE)
    folded = jnp.zeros((2, GRID_SIDE, GRID_SIDE), jnp.float32)
    for shift_u in range(PATCH):
        for shift_v in range(PATCH):
            folded = folded + jnp.roll(pieces[:, shift_u, shift_v], (shift_u, shift_v), axis=(1, 2))
    return folded


def reference(voltages, anchor_u_cells, anchor_v_cells, tile_kernel_offsets, kernel_u, kernel_v):
    def per_channel(operands):
        volts, cell_u, cell_v, offsets = operands
        cell_ids = (cell_u * GRID_SIDE + cell_v).astype(jnp.int32)
        volts_wide = volts.astype(jnp.float32)
        left_side = jnp.concatenate([volts_wide, jnp.concatenate([volts_wide[:, SAMPLE_COUNT:], -volts_wide[:, :SAMPLE_COUNT]], axis=1)], axis=0)
        gram = jnp.dot(left_side, volts_wide.T, precision=lax.Precision.HIGHEST)
        vis = (gram * (1.0 / SAMPLE_COUNT)).astype(jnp.bfloat16)
        tally_count = INPUT_COUNT // TILE_SIDE
        vis_tiles = vis.reshape(2, tally_count, TILE_SIDE, tally_count, TILE_SIDE).transpose(0, 2, 4, 1, 3)
        step_rows = min(64, tally_count)

        def accumulate(block_index, patched):
            start = (block_index * step_rows).astype(jnp.int32)
            block = lax.dynamic_slice_in_dim(vis_tiles, start, step_rows, 3).astype(jnp.float32)
            block = block.reshape(2, TILE_SIDE, TILE_SIDE, step_rows * tally_count)
            cell_block = lax.dynamic_slice_in_dim(cell_ids, start, step_rows, 0).reshape(-1)
            offset_block = lax.dynamic_slice_in_dim(offsets, start, step_rows, 0).reshape(-1)
            kern_left = kernel_u[offset_block // KERNEL_STEPS].T.reshape(PATCH, TILE_SIDE, -1)
            kern_right = kernel_v[offset_block % KERNEL_STEPS].T.reshape(PATCH, TILE_SIDE, -1)
            return patched.at[:, cell_block].add(tile_patches(block, kern_left, kern_right))

        patched = lax.fori_loop(0, tally_count // step_rows, accumulate, jnp.zeros((2 * PATCH * PATCH, GRID_SIDE * GRID_SIDE), jnp.float32))
        return fold_grid(patched)

    return lax.map(per_channel, (voltages, anchor_u_cells, anchor_v_cells, tile_kernel_offsets))
```

```python
import functools

import jax
import jax.numpy as jnp
from jax import lax
from jax.experimental import pallas as pl
from jax.experimental.pallas import tpu as pltpu
from jax.sharding import PartitionSpec as P

TILE_SIDE = 4
PATCH = 8
KERNEL_STEPS = 8
GRID_SIDE = 256
STEP_ROWS = 32


def rolled_table(kernel):
    table = kernel.reshape(KERNEL_STEPS, PATCH, TILE_SIDE)
    rolled = jnp.stack([jnp.roll(table, shift, axis=1) for shift in range(PATCH)], axis=1)
    return rolled.transpose(3, 2, 0, 1).reshape(TILE_SIDE * PATCH, KERNEL_STEPS * PATCH)


def grid_kernel(scale, left_ref, cols_ref, au_ref, av_ref, off_ref, table_ref, out_ref, vis, spread_v, spread_u):
    tile_cols = cols_ref.shape[0] // TILE_SIDE
    kinds = KERNEL_STEPS * PATCH
    bands = GRID_SIDE // PATCH
    step = pl.program_id(0)

    def multiply(slot):
        out_ref[...] += lax.dot_general(
            spread_v[slot], spread_u[slot], (((1,), (1,)), ((), ())), preferred_element_type=jnp.float32
        )

    def place(slot_ref, anchor, pieces):
        row = lax.broadcasted_iota(jnp.int32, (2 * PATCH, tile_cols), 0)
        low = anchor & (PATCH - 1)
        band = ((anchor >> 3) + ((row & (PATCH - 1)) < low).astype(jnp.int32)) & (bands - 1)
        band = (band - (row >> 3)).astype(jnp.float32).astype(jnp.bfloat16)
        for block in range(bands // 2):
            hit = band == jnp.bfloat16(2 * block)
            for plane, index_k, piece in pieces:
                start = plane * GRID_SIDE + block * 2 * PATCH
                slot_ref[start : start + 2 * PATCH, index_k * tile_cols : (index_k + 1) * tile_cols] = jnp.where(
                    hit, piece, jnp.bfloat16(0)
                )

    def build(slot, s):
        av = av_ref[pl.ds(s, 1), :]
        au = au_ref[pl.ds(s, 1), :]
        off = off_ref[pl.ds(s, 1), :]
        kind = lax.broadcasted_iota(jnp.int32, (kinds, tile_cols), 0)
        pick_v = (kind == (off & (KERNEL_STEPS - 1)) * PATCH + (av & (PATCH - 1))).astype(jnp.float32)
        pick_u = (kind == (off >> 3) * PATCH + (au & (PATCH - 1))).astype(jnp.float32)
        pick = jnp.concatenate([pick_v, pick_u], axis=0).astype(jnp.bfloat16)
        chosen = jnp.dot(table_ref[...], pick, preferred_element_type=jnp.float32)
        span = TILE_SIDE * PATCH
        kern_v = chosen[:span] + chosen[span : 2 * span]
        kern_u = chosen[2 * span :]
        pieces = []
        for index_k in range(TILE_SIDE):
            for plane in range(2):
                total = None
                for index_l in range(TILE_SIDE):
                    base = (plane * TILE_SIDE + index_k) * STEP_ROWS
                    value = vis[pl.ds(base + s, 1), index_l * tile_cols : (index_l + 1) * tile_cols]
                    term = value * kern_v[index_l * PATCH : (index_l + 1) * PATCH]
                    total = term if total is None else total + term
                pieces.append((plane, index_k, jnp.concatenate([total, total], axis=0).astype(jnp.bfloat16)))
        place(spread_v.at[slot], av, pieces)
        pieces = []
        for index_k in range(TILE_SIDE):
            piece = kern_u[index_k * PATCH : (index_k + 1) * PATCH]
            pieces.append((0, index_k, jnp.concatenate([piece, piece], axis=0).astype(jnp.bfloat16)))
        place(spread_u.at[slot], au, pieces)

    @pl.when(step == 0)
    def _():
        out_ref[...] = jnp.zeros_like(out_ref)
        spread_v[1] = jnp.zeros(spread_v.shape[1:], spread_v.dtype)
        spread_u[1] = jnp.zeros(spread_u.shape[1:], spread_u.dtype)

    for index_l in range(TILE_SIDE):
        part = slice(index_l * tile_cols, (index_l + 1) * tile_cols)
        gram = lax.dot_general(
            left_ref[0], cols_ref[part], (((1,), (1,)), ((), ())), preferred_element_type=jnp.float32
        )
        vis[:, part] = (gram * scale).astype(jnp.bfloat16).astype(jnp.float32)

    def pair(index, carry):
        build(0, 2 * index)
        multiply(1)
        build(1, 2 * index + 1)
        multiply(0)
        return carry

    lax.fori_loop(0, STEP_ROWS // 2, pair, 0)

    @pl.when(step == pl.num_programs(0) - 1)
    def _():
        multiply(1)


def grid_tiles(left, cols, au, av, off, table, scale):
    steps, left_rows, width = left.shape
    tile_cols = au.shape[1]
    depth = TILE_SIDE * tile_cols
    whole = lambda i: (0, 0)
    return pl.pallas_call(
        functools.partial(grid_kernel, scale),
        grid=(steps,),
        in_specs=[
            pl.BlockSpec((1, left_rows, width), lambda i: (i, 0, 0)),
            pl.BlockSpec(cols.shape, whole),
            pl.BlockSpec((STEP_ROWS, tile_cols), lambda i: (i, 0)),
            pl.BlockSpec((STEP_ROWS, tile_cols), lambda i: (i, 0)),
            pl.BlockSpec((STEP_ROWS, tile_cols), lambda i: (i, 0)),
            pl.BlockSpec(table.shape, whole),
        ],
        out_specs=pl.BlockSpec((2 * GRID_SIDE, GRID_SIDE), whole),
        out_shape=jax.ShapeDtypeStruct((2 * GRID_SIDE, GRID_SIDE), jnp.float32),
        scratch_shapes=[
            pltpu.VMEM((left_rows, depth), jnp.float32),
            pltpu.VMEM((2, 2 * GRID_SIDE, depth), jnp.bfloat16),
            pltpu.VMEM((2, GRID_SIDE, depth), jnp.bfloat16),
        ],
        compiler_params=pltpu.CompilerParams(vmem_limit_bytes=48 * 1024 * 1024),
    )(left, cols, au, av, off, table)


def body(voltages, anchor_u_cells, anchor_v_cells, tile_kernel_offsets, kernel_u, kernel_v):
    samples = voltages.shape[2] // 2
    n_rows = lax.axis_size("row")
    n_cols = lax.axis_size("col")
    n_chan = lax.axis_size("chan")
    shard_depth = voltages.shape[1]
    turned = lax.all_to_all(voltages, "chan", split_axis=0, concat_axis=1, tiled=True)
    local_chan = turned.shape[0]
    width = 2 * samples
    spread = lax.all_gather(turned, ("row", "col"), axis=1, tiled=True)
    all_volts = spread.reshape(local_chan, n_rows * n_cols, n_chan, shard_depth, width)
    all_volts = all_volts.transpose(0, 2, 1, 3, 4).reshape(
        local_chan, n_rows * n_cols * n_chan * shard_depth, width
    )
    row_count = all_volts.shape[1] // n_rows
    col_count = all_volts.shape[1] // n_cols
    row_volts = lax.dynamic_slice_in_dim(all_volts, lax.axis_index("row") * row_count, row_count, 1)
    col_volts = lax.dynamic_slice_in_dim(all_volts, lax.axis_index("col") * col_count, col_count, 1)
    tile_rows = row_count // TILE_SIDE
    tile_cols = col_count // TILE_SIDE
    steps = tile_rows // STEP_ROWS
    rows = row_volts[0].reshape(steps, STEP_ROWS, TILE_SIDE, width).transpose(0, 2, 1, 3)
    rows = rows.reshape(steps, TILE_SIDE * STEP_ROWS, width)
    turned_rows = jnp.concatenate([rows[..., samples:], -rows[..., :samples]], axis=2)
    left = jnp.concatenate([rows, turned_rows], axis=1)
    cols = col_volts[0].reshape(tile_cols, TILE_SIDE, width).transpose(1, 0, 2).reshape(col_count, width)
    table_v = rolled_table(kernel_v)
    table_u = rolled_table(kernel_u)
    high_v = table_v.astype(jnp.bfloat16).astype(jnp.float32)
    none = jnp.zeros_like(table_v)
    table = jnp.concatenate(
        [
            jnp.concatenate([high_v, none], axis=1),
            jnp.concatenate([table_v - high_v, none], axis=1),
            jnp.concatenate([none, table_u], axis=1),
        ],
        axis=0,
    ).astype(jnp.bfloat16)
    gridded = grid_tiles(
        left, cols, anchor_u_cells[0], anchor_v_cells[0], tile_kernel_offsets[0], table, 1.0 / samples
    )
    folded = gridded.reshape(1, 2, GRID_SIDE, GRID_SIDE).transpose(0, 1, 3, 2)
    return lax.psum_scatter(folded, ("row", "col"), scatter_dimension=2, tiled=True)


def solution(mesh):
    in_specs = (
        P(None, ("chan", "row", "col"), None),
        P("chan", "row", "col"),
        P("chan", "row", "col"),
        P("chan", "row", "col"),
        P(),
        P(),
    )
    out_specs = P("chan", None, ("row", "col"), None)
    return jax.shard_map(body, mesh=mesh, in_specs=in_specs, out_specs=out_specs, check_vma=False)
```

```python
import functools

import jax
import jax.numpy as jnp
from jax import lax
from jax.experimental import pallas as pl
from jax.experimental.pallas import tpu as pltpu
from jax.sharding import PartitionSpec as P

TILE_SIDE = 4
PATCH = 8
KERNEL_STEPS = 8
GRID_SIDE = 256
STEP_ROWS = 32
GROUP = 4


def rolled_table(kernel):
    table = kernel.reshape(KERNEL_STEPS, PATCH, TILE_SIDE)
    rolled = jnp.stack([jnp.roll(table, shift, axis=1) for shift in range(PATCH)], axis=1)
    return rolled.transpose(3, 2, 0, 1).reshape(TILE_SIDE * PATCH, KERNEL_STEPS * PATCH)


def grid_kernel(scale, left_ref, cols_ref, au_ref, av_ref, off_ref, table_ref, out_ref, vis, spread_v, spread_u, acc):
    tile_cols = cols_ref.shape[0] // TILE_SIDE
    kinds = KERNEL_STEPS * PATCH
    bands = GRID_SIDE // PATCH
    step = pl.program_id(0)

    def multiply():
        acc[...] += lax.dot_general(
            spread_v[...], spread_u[...], (((1,), (1,)), ((), ())), preferred_element_type=jnp.float32
        )

    def place(slot_ref, base, anchor, pieces):
        row = lax.broadcasted_iota(jnp.int32, (2 * PATCH, tile_cols), 0)
        low = anchor & (PATCH - 1)
        band = ((anchor >> 3) + ((row & (PATCH - 1)) < low).astype(jnp.int32)) & (bands - 1)
        band = (band - (row >> 3)).astype(jnp.float32).astype(jnp.bfloat16)
        for block in range(bands // 2):
            hit = band == jnp.bfloat16(2 * block)
            for plane, index_k, piece in pieces:
                start = plane * GRID_SIDE + block * 2 * PATCH
                slot_ref[start : start + 2 * PATCH, pl.ds(base + index_k * tile_cols, tile_cols)] = jnp.where(
                    hit, piece, jnp.bfloat16(0)
                )

    def build(lane, s):
        av = av_ref[pl.ds(s, 1), :]
        au = au_ref[pl.ds(s, 1), :]
        off = off_ref[pl.ds(s, 1), :]
        kind = lax.broadcasted_iota(jnp.int32, (kinds, tile_cols), 0)
        pick_v = (kind == (off & (KERNEL_STEPS - 1)) * PATCH + (av & (PATCH - 1))).astype(jnp.float32)
        pick_u = (kind == (off >> 3) * PATCH + (au & (PATCH - 1))).astype(jnp.float32)
        pick = jnp.concatenate([pick_v, pick_u], axis=0).astype(jnp.bfloat16)
        chosen = jnp.dot(table_ref[...], pick, preferred_element_type=jnp.float32)
        span = TILE_SIDE * PATCH
        kern_v = chosen[:span] + chosen[span : 2 * span]
        kern_u = chosen[2 * span :]
        pieces = []
        for index_k in range(TILE_SIDE):
            for plane in range(2):
                total = None
                for index_l in range(TILE_SIDE):
                    base = (plane * TILE_SIDE + index_k) * STEP_ROWS
                    value = vis[pl.ds(base + s, 1), index_l * tile_cols : (index_l + 1) * tile_cols]
                    term = value * kern_v[index_l * PATCH : (index_l + 1) * PATCH]
                    total = term if total is None else total + term
                pieces.append((plane, index_k, jnp.concatenate([total, total], axis=0).astype(jnp.bfloat16)))
        place(spread_v, lane, av, pieces)
        pieces = []
        for index_k in range(TILE_SIDE):
            piece = kern_u[index_k * PATCH : (index_k + 1) * PATCH]
            pieces.append((0, index_k, jnp.concatenate([piece, piece], axis=0).astype(jnp.bfloat16)))
        place(spread_u, lane, au, pieces)

    @pl.when(step == 0)
    def _():
        acc[...] = jnp.zeros_like(acc)

    for index_l in range(TILE_SIDE):
        part = slice(index_l * tile_cols, (index_l + 1) * tile_cols)
        gram = lax.dot_general(
            left_ref[0], cols_ref[part], (((1,), (1,)), ((), ())), preferred_element_type=jnp.float32
        )
        vis[:, part] = (gram * scale).astype(jnp.bfloat16).astype(jnp.float32)

    depth = TILE_SIDE * tile_cols

    def group(index, carry):
        def one(j, carry):
            build(pl.multiple_of(j * depth, depth), index * GROUP + j)
            return carry

        for j in range(GROUP):
            build(j * depth, index * GROUP + j)
        multiply()
        return carry

    lax.fori_loop(0, STEP_ROWS // GROUP, group, 0)

    @pl.when(step == pl.num_programs(0) - 1)
    def _():
        out_ref[...] = acc[...]


def grid_tiles(left, cols, au, av, off, table, scale):
    steps, left_rows, width = left.shape
    tile_cols = au.shape[1]
    depth = TILE_SIDE * tile_cols
    whole = lambda i: (0, 0)
    return pl.pallas_call(
        functools.partial(grid_kernel, scale),
        grid=(steps,),
        in_specs=[
            pl.BlockSpec((1, left_rows, width), lambda i: (i, 0, 0)),
            pl.BlockSpec(cols.shape, whole),
            pl.BlockSpec((STEP_ROWS, tile_cols), lambda i: (i, 0)),
            pl.BlockSpec((STEP_ROWS, tile_cols), lambda i: (i, 0)),
            pl.BlockSpec((STEP_ROWS, tile_cols), lambda i: (i, 0)),
            pl.BlockSpec(table.shape, whole),
        ],
        out_specs=pl.BlockSpec((2 * GRID_SIDE, GRID_SIDE), whole),
        out_shape=jax.ShapeDtypeStruct((2 * GRID_SIDE, GRID_SIDE), jnp.float32),
        scratch_shapes=[
            pltpu.VMEM((left_rows, depth), jnp.float32),
            pltpu.VMEM((2 * GRID_SIDE, GROUP * depth), jnp.bfloat16),
            pltpu.VMEM((GRID_SIDE, GROUP * depth), jnp.bfloat16),
            pltpu.VMEM((2 * GRID_SIDE, GRID_SIDE), jnp.float32),
        ],
        compiler_params=pltpu.CompilerParams(vmem_limit_bytes=48 * 1024 * 1024),
    )(left, cols, au, av, off, table)


def body(voltages, anchor_u_cells, anchor_v_cells, tile_kernel_offsets, kernel_u, kernel_v):
    samples = voltages.shape[2] // 2
    n_rows = lax.axis_size("row")
    n_cols = lax.axis_size("col")
    n_chan = lax.axis_size("chan")
    shard_depth = voltages.shape[1]
    turned = lax.all_to_all(voltages, "chan", split_axis=0, concat_axis=1, tiled=True)
    local_chan = turned.shape[0]
    width = 2 * samples
    spread = lax.all_gather(turned, ("row", "col"), axis=1, tiled=True)
    all_volts = spread.reshape(local_chan, n_rows * n_cols, n_chan, shard_depth, width)
    all_volts = all_volts.transpose(0, 2, 1, 3, 4).reshape(
        local_chan, n_rows * n_cols * n_chan * shard_depth, width
    )
    row_count = all_volts.shape[1] // n_rows
    col_count = all_volts.shape[1] // n_cols
    row_volts = lax.dynamic_slice_in_dim(all_volts, lax.axis_index("row") * row_count, row_count, 1)
    col_volts = lax.dynamic_slice_in_dim(all_volts, lax.axis_index("col") * col_count, col_count, 1)
    tile_rows = row_count // TILE_SIDE
    tile_cols = col_count // TILE_SIDE
    steps = tile_rows // STEP_ROWS
    rows = row_volts[0].reshape(steps, STEP_ROWS, TILE_SIDE, width).transpose(0, 2, 1, 3)
    rows = rows.reshape(steps, TILE_SIDE * STEP_ROWS, width)
    turned_rows = jnp.concatenate([rows[..., samples:], -rows[..., :samples]], axis=2)
    left = jnp.concatenate([rows, turned_rows], axis=1)
    cols = col_volts[0].reshape(tile_cols, TILE_SIDE, width).transpose(1, 0, 2).reshape(col_count, width)
    table_v = rolled_table(kernel_v)
    table_u = rolled_table(kernel_u)
    high_v = lax.reduce_precision(table_v, 8, 7)
    none = jnp.zeros_like(table_v)
    table = jnp.concatenate(
        [
            jnp.concatenate([high_v, none], axis=1),
            jnp.concatenate([table_v - high_v, none], axis=1),
            jnp.concatenate([none, table_u], axis=1),
        ],
        axis=0,
    ).astype(jnp.bfloat16)
    gridded = grid_tiles(
        left, cols, anchor_u_cells[0], anchor_v_cells[0], tile_kernel_offsets[0], table, 1.0 / samples
    )
    folded = gridded.reshape(1, 2, GRID_SIDE, GRID_SIDE).transpose(0, 1, 3, 2)
    return lax.psum_scatter(folded, ("row", "col"), scatter_dimension=2, tiled=True)


def solution(mesh):
    in_specs = (
        P(None, ("chan", "row", "col"), None),
        P("chan", "row", "col"),
        P("chan", "row", "col"),
        P("chan", "row", "col"),
        P(),
        P(),
    )
    out_specs = P("chan", None, ("row", "col"), None)
    return jax.shard_map(body, mesh=mesh, in_specs=in_specs, out_specs=out_specs, check_vma=False)
```

```python
import functools

import jax
import jax.numpy as jnp
from jax import lax
from jax.experimental import pallas as pl
from jax.experimental.pallas import tpu as pltpu
from jax.sharding import PartitionSpec as P

TILE_SIDE = 4
PATCH = 8
KERNEL_STEPS = 8
GRID_SIDE = 256
STEP_ROWS = 32
GROUP = 8


def rolled_table(kernel):
    table = kernel.reshape(KERNEL_STEPS, PATCH, TILE_SIDE)
    rolled = jnp.stack([jnp.roll(table, shift, axis=1) for shift in range(PATCH)], axis=1)
    return rolled.transpose(3, 2, 0, 1).reshape(TILE_SIDE * PATCH, KERNEL_STEPS * PATCH)


def grid_kernel(scale, left_ref, cols_ref, au_ref, av_ref, off_ref, table_ref, out_ref, vis, spread_v, spread_u, acc):
    tile_cols = cols_ref.shape[0] // TILE_SIDE
    kinds = KERNEL_STEPS * PATCH
    bands = GRID_SIDE // PATCH
    step = pl.program_id(0)

    def multiply():
        acc[...] += lax.dot_general(
            spread_v[...], spread_u[...], (((1,), (1,)), ((), ())), preferred_element_type=jnp.float32
        )

    def place(slot_ref, base, anchor, pieces):
        row = lax.broadcasted_iota(jnp.int32, (2 * PATCH, tile_cols), 0)
        low = anchor & (PATCH - 1)
        band = ((anchor >> 3) + ((row & (PATCH - 1)) < low).astype(jnp.int32)) & (bands - 1)
        band = (band - (row >> 3)).astype(jnp.float32).astype(jnp.bfloat16)
        for block in range(bands // 2):
            hit = band == jnp.bfloat16(2 * block)
            for plane, index_k, piece in pieces:
                start = plane * GRID_SIDE + block * 2 * PATCH
                slot_ref[start : start + 2 * PATCH, pl.ds(base + index_k * tile_cols, tile_cols)] = jnp.where(
                    hit, piece, jnp.bfloat16(0)
                )

    def build(lane, s):
        av = av_ref[pl.ds(s, 1), :]
        au = au_ref[pl.ds(s, 1), :]
        off = off_ref[pl.ds(s, 1), :]
        kind = lax.broadcasted_iota(jnp.int32, (kinds, tile_cols), 0)
        pick_v = (kind == (off & (KERNEL_STEPS - 1)) * PATCH + (av & (PATCH - 1))).astype(jnp.float32)
        pick_u = (kind == (off >> 3) * PATCH + (au & (PATCH - 1))).astype(jnp.float32)
        pick = jnp.concatenate([pick_v, pick_u], axis=0).astype(jnp.bfloat16)
        chosen = jnp.dot(table_ref[...], pick, preferred_element_type=jnp.float32)
        span = TILE_SIDE * PATCH
        kern_v = chosen[:span] + chosen[span : 2 * span]
        kern_u = chosen[2 * span :]
        pieces = []
        for index_k in range(TILE_SIDE):
            for plane in range(2):
                total = None
                for index_l in range(TILE_SIDE):
                    base = (plane * TILE_SIDE + index_k) * STEP_ROWS
                    value = vis[pl.ds(base + s, 1), index_l * tile_cols : (index_l + 1) * tile_cols]
                    term = value * kern_v[index_l * PATCH : (index_l + 1) * PATCH]
                    total = term if total is None else total + term
                pieces.append((plane, index_k, jnp.concatenate([total, total], axis=0).astype(jnp.bfloat16)))
        place(spread_v, lane, av, pieces)
        pieces = []
        for index_k in range(TILE_SIDE):
            piece = kern_u[index_k * PATCH : (index_k + 1) * PATCH]
            pieces.append((0, index_k, jnp.concatenate([piece, piece], axis=0).astype(jnp.bfloat16)))
        place(spread_u, lane, au, pieces)

    @pl.when(step == 0)
    def _():
        acc[...] = jnp.zeros_like(acc)

    for index_l in range(TILE_SIDE):
        part = slice(index_l * tile_cols, (index_l + 1) * tile_cols)
        gram = lax.dot_general(
            left_ref[0], cols_ref[part], (((1,), (1,)), ((), ())), preferred_element_type=jnp.float32
        )
        vis[:, part] = (gram * scale).astype(jnp.bfloat16).astype(jnp.float32)

    depth = TILE_SIDE * tile_cols

    def group(index, carry):
        def one(j, carry):
            build(pl.multiple_of(j * depth, depth), index * GROUP + j)
            return carry

        for j in range(GROUP):
            build(j * depth, index * GROUP + j)
        multiply()
        return carry

    lax.fori_loop(0, STEP_ROWS // GROUP, group, 0)

    @pl.when(step == pl.num_programs(0) - 1)
    def _():
        out_ref[...] = acc[...]


def grid_tiles(left, cols, au, av, off, table, scale):
    steps, left_rows, width = left.shape
    tile_cols = au.shape[1]
    depth = TILE_SIDE * tile_cols
    whole = lambda i: (0, 0)
    return pl.pallas_call(
        functools.partial(grid_kernel, scale),
        grid=(steps,),
        in_specs=[
            pl.BlockSpec((1, left_rows, width), lambda i: (i, 0, 0)),
            pl.BlockSpec(cols.shape, whole),
            pl.BlockSpec((STEP_ROWS, tile_cols), lambda i: (i, 0)),
            pl.BlockSpec((STEP_ROWS, tile_cols), lambda i: (i, 0)),
            pl.BlockSpec((STEP_ROWS, tile_cols), lambda i: (i, 0)),
            pl.BlockSpec(table.shape, whole),
        ],
        out_specs=pl.BlockSpec((2 * GRID_SIDE, GRID_SIDE), whole),
        out_shape=jax.ShapeDtypeStruct((2 * GRID_SIDE, GRID_SIDE), jnp.float32),
        scratch_shapes=[
            pltpu.VMEM((left_rows, depth), jnp.float32),
            pltpu.VMEM((2 * GRID_SIDE, GROUP * depth), jnp.bfloat16),
            pltpu.VMEM((GRID_SIDE, GROUP * depth), jnp.bfloat16),
            pltpu.VMEM((2 * GRID_SIDE, GRID_SIDE), jnp.float32),
        ],
        compiler_params=pltpu.CompilerParams(vmem_limit_bytes=48 * 1024 * 1024),
    )(left, cols, au, av, off, table)


def scatter_kernel(n_rows, n_cols, parts_ref, out_ref, landed, send_sems, recv_sems):
    peers = n_rows * n_cols
    band = out_ref.shape[2]
    me = lax.axis_index("row") * n_cols + lax.axis_index("col")
    barrier = pltpu.get_barrier_semaphore()

    def place_of(offset):
        peer = lax.rem(me + offset, peers)
        return peer, {"row": peer // n_cols, "col": lax.rem(peer, n_cols)}

    for offset in range(1, peers):
        pl.semaphore_signal(barrier, inc=1, device_id=place_of(offset)[1], device_id_type=pl.DeviceIdType.MESH)
    pl.semaphore_wait(barrier, peers - 1)
    copies = []
    for offset in range(1, peers):
        peer, place = place_of(offset)
        copy = pltpu.make_async_remote_copy(
            src_ref=parts_ref.at[:, :, pl.ds(pl.multiple_of(peer * band, band), band), :],
            dst_ref=landed.at[offset - 1],
            send_sem=send_sems.at[offset - 1],
            recv_sem=recv_sems.at[offset - 1],
            device_id=place,
            device_id_type=pl.DeviceIdType.MESH,
        )
        copy.start()
        copies.append(copy)
    total = parts_ref[:, :, pl.ds(pl.multiple_of(me * band, band), band), :]
    for index, copy in enumerate(copies):
        copy.wait_recv()
        total = total + landed[index]
    out_ref[...] = total
    for copy in copies:
        copy.wait_send()


def scatter_sum(parts):
    n_rows = lax.axis_size("row")
    n_cols = lax.axis_size("col")
    peers = n_rows * n_cols
    shape = (parts.shape[0], parts.shape[1], parts.shape[2] // peers, parts.shape[3])
    return pl.pallas_call(
        functools.partial(scatter_kernel, n_rows, n_cols),
        in_specs=[pl.BlockSpec(memory_space=pltpu.VMEM)],
        out_specs=pl.BlockSpec(memory_space=pltpu.VMEM),
        out_shape=jax.ShapeDtypeStruct(shape, jnp.float32),
        scratch_shapes=[
            pltpu.VMEM((peers - 1,) + shape, jnp.float32),
            pltpu.SemaphoreType.DMA((peers - 1,)),
            pltpu.SemaphoreType.DMA((peers - 1,)),
        ],
        compiler_params=pltpu.CompilerParams(
            collective_id=0, has_side_effects=True, vmem_limit_bytes=16 * 1024 * 1024
        ),
    )(parts)


def body(voltages, anchor_u_cells, anchor_v_cells, tile_kernel_offsets, kernel_u, kernel_v):
    samples = voltages.shape[2] // 2
    n_rows = lax.axis_size("row")
    n_cols = lax.axis_size("col")
    n_chan = lax.axis_size("chan")
    shard_depth = voltages.shape[1]
    turned = lax.all_to_all(voltages, "chan", split_axis=0, concat_axis=1, tiled=True)
    local_chan = turned.shape[0]
    width = 2 * samples
    spread = lax.all_gather(turned, ("row", "col"), axis=1, tiled=True)
    all_volts = spread.reshape(local_chan, n_rows * n_cols, n_chan, shard_depth, width)
    all_volts = all_volts.transpose(0, 2, 1, 3, 4).reshape(
        local_chan, n_rows * n_cols * n_chan * shard_depth, width
    )
    row_count = all_volts.shape[1] // n_rows
    col_count = all_volts.shape[1] // n_cols
    row_volts = lax.dynamic_slice_in_dim(all_volts, lax.axis_index("row") * row_count, row_count, 1)
    col_volts = lax.dynamic_slice_in_dim(all_volts, lax.axis_index("col") * col_count, col_count, 1)
    tile_rows = row_count // TILE_SIDE
    tile_cols = col_count // TILE_SIDE
    steps = tile_rows // STEP_ROWS
    rows = row_volts[0].reshape(steps, STEP_ROWS, TILE_SIDE, width).transpose(0, 2, 1, 3)
    rows = rows.reshape(steps, TILE_SIDE * STEP_ROWS, width)
    turned_rows = jnp.concatenate([rows[..., samples:], -rows[..., :samples]], axis=2)
    left = jnp.concatenate([rows, turned_rows], axis=1)
    cols = col_volts[0].reshape(tile_cols, TILE_SIDE, width).transpose(1, 0, 2).reshape(col_count, width)
    table_v = rolled_table(kernel_v)
    table_u = rolled_table(kernel_u)
    high_v = lax.reduce_precision(table_v, 8, 7)
    none = jnp.zeros_like(table_v)
    table = jnp.concatenate(
        [
            jnp.concatenate([high_v, none], axis=1),
            jnp.concatenate([table_v - high_v, none], axis=1),
            jnp.concatenate([none, table_u], axis=1),
        ],
        axis=0,
    ).astype(jnp.bfloat16)
    gridded = grid_tiles(
        left, cols, anchor_u_cells[0], anchor_v_cells[0], tile_kernel_offsets[0], table, 1.0 / samples
    )
    folded = gridded.reshape(1, 2, GRID_SIDE, GRID_SIDE).transpose(0, 1, 3, 2)
    return scatter_sum(folded)


def solution(mesh):
    in_specs = (
        P(None, ("chan", "row", "col"), None),
        P("chan", "row", "col"),
        P("chan", "row", "col"),
        P("chan", "row", "col"),
        P(),
        P(),
    )
    out_specs = P("chan", None, ("row", "col"), None)
    return jax.shard_map(body, mesh=mesh, in_specs=in_specs, out_specs=out_specs, check_vma=False)
```

```python
import functools

import jax
import jax.numpy as jnp
from jax import lax
from jax.experimental import pallas as pl
from jax.experimental.pallas import tpu as pltpu
from jax.sharding import PartitionSpec as P

TILE_SIDE = 4
PATCH = 8
KERNEL_STEPS = 8
GRID_SIDE = 256
STEP_ROWS = 32
GROUP = 8


def rolled_table(kernel):
    table = kernel.reshape(KERNEL_STEPS, PATCH, TILE_SIDE)
    rolled = jnp.stack([jnp.roll(table, shift, axis=1) for shift in range(PATCH)], axis=1)
    return rolled.transpose(3, 2, 0, 1).reshape(TILE_SIDE * PATCH, KERNEL_STEPS * PATCH)


def grid_kernel(scale, left_ref, cols_ref, au_ref, av_ref, off_ref, table_ref, out_ref, vis, spread_v, spread_u, acc):
    tile_cols = cols_ref.shape[0] // TILE_SIDE
    kinds = KERNEL_STEPS * PATCH
    bands = GRID_SIDE // PATCH
    step = pl.program_id(0)

    def multiply():
        acc[...] += lax.dot_general(
            spread_v[...], spread_u[...], (((1,), (1,)), ((), ())), preferred_element_type=jnp.float32
        )

    def place(slot_ref, base, anchor, pieces):
        row = lax.broadcasted_iota(jnp.int32, (2 * PATCH, tile_cols), 0)
        low = anchor & (PATCH - 1)
        band = ((anchor >> 3) + ((row & (PATCH - 1)) < low).astype(jnp.int32)) & (bands - 1)
        band = (band - (row >> 3)).astype(jnp.float32).astype(jnp.bfloat16)
        for block in range(bands // 2):
            hit = band == jnp.bfloat16(2 * block)
            for plane, index_k, piece in pieces:
                start = plane * GRID_SIDE + block * 2 * PATCH
                slot_ref[start : start + 2 * PATCH, pl.ds(base + index_k * tile_cols, tile_cols)] = jnp.where(
                    hit, piece, jnp.bfloat16(0)
                )

    def build(lane, s):
        av = av_ref[pl.ds(s, 1), :]
        au = au_ref[pl.ds(s, 1), :]
        off = off_ref[pl.ds(s, 1), :]
        kind = lax.broadcasted_iota(jnp.int32, (kinds, tile_cols), 0)
        pick_v = (kind == (off & (KERNEL_STEPS - 1)) * PATCH + (av & (PATCH - 1))).astype(jnp.float32)
        pick_u = (kind == (off >> 3) * PATCH + (au & (PATCH - 1))).astype(jnp.float32)
        pick = jnp.concatenate([pick_v, pick_u], axis=0).astype(jnp.bfloat16)
        chosen = jnp.dot(table_ref[...], pick, preferred_element_type=jnp.float32)
        span = TILE_SIDE * PATCH
        kern_v = chosen[:span] + chosen[span : 2 * span]
        kern_u = chosen[2 * span :]
        pieces = []
        for index_k in range(TILE_SIDE):
            for plane in range(2):
                total = None
                for index_l in range(TILE_SIDE):
                    base = (plane * TILE_SIDE + index_k) * STEP_ROWS
                    value = vis[pl.ds(base + s, 1), index_l * tile_cols : (index_l + 1) * tile_cols]
                    term = value * kern_v[index_l * PATCH : (index_l + 1) * PATCH]
                    total = term if total is None else total + term
                pieces.append((plane, index_k, jnp.concatenate([total, total], axis=0).astype(jnp.bfloat16)))
        place(spread_v, lane, av, pieces)
        pieces = []
        for index_k in range(TILE_SIDE):
            piece = kern_u[index_k * PATCH : (index_k + 1) * PATCH]
            pieces.append((0, index_k, jnp.concatenate([piece, piece], axis=0).astype(jnp.bfloat16)))
        place(spread_u, lane, au, pieces)

    @pl.when(step == 0)
    def _():
        acc[...] = jnp.zeros_like(acc)

    for index_l in range(TILE_SIDE):
        part = slice(index_l * tile_cols, (index_l + 1) * tile_cols)
        gram = lax.dot_general(
            left_ref[0], cols_ref[part], (((1,), (1,)), ((), ())), preferred_element_type=jnp.float32
        )
        vis[:, part] = (gram * scale).astype(jnp.bfloat16).astype(jnp.float32)

    depth = TILE_SIDE * tile_cols

    def group(index, carry):
        def one(j, carry):
            build(pl.multiple_of(j * depth, depth), index * GROUP + j)
            return carry

        for j in range(GROUP):
            build(j * depth, index * GROUP + j)
        multiply()
        return carry

    lax.fori_loop(0, STEP_ROWS // GROUP, group, 0)

    @pl.when(step == pl.num_programs(0) - 1)
    def _():
        out_ref[...] = acc[...]


def grid_tiles(left, cols, au, av, off, table, scale):
    steps, left_rows, width = left.shape
    tile_cols = au.shape[1]
    depth = TILE_SIDE * tile_cols
    whole = lambda i: (0, 0)
    return pl.pallas_call(
        functools.partial(grid_kernel, scale),
        grid=(steps,),
        in_specs=[
            pl.BlockSpec((1, left_rows, width), lambda i: (i, 0, 0)),
            pl.BlockSpec(cols.shape, whole),
            pl.BlockSpec((STEP_ROWS, tile_cols), lambda i: (i, 0)),
            pl.BlockSpec((STEP_ROWS, tile_cols), lambda i: (i, 0)),
            pl.BlockSpec((STEP_ROWS, tile_cols), lambda i: (i, 0)),
            pl.BlockSpec(table.shape, whole),
        ],
        out_specs=pl.BlockSpec((2 * GRID_SIDE, GRID_SIDE), whole),
        out_shape=jax.ShapeDtypeStruct((2 * GRID_SIDE, GRID_SIDE), jnp.float32),
        scratch_shapes=[
            pltpu.VMEM((left_rows, depth), jnp.float32),
            pltpu.VMEM((2 * GRID_SIDE, GROUP * depth), jnp.bfloat16),
            pltpu.VMEM((GRID_SIDE, GROUP * depth), jnp.bfloat16),
            pltpu.VMEM((2 * GRID_SIDE, GRID_SIDE), jnp.float32),
        ],
        compiler_params=pltpu.CompilerParams(vmem_limit_bytes=48 * 1024 * 1024),
    )(left, cols, au, av, off, table)


def scatter_kernel(n_rows, n_cols, parts_ref, out_ref, landed, send_sems, recv_sems):
    peers = n_rows * n_cols
    band = out_ref.shape[2]
    me = lax.axis_index("row") * n_cols + lax.axis_index("col")
    barrier = pltpu.get_barrier_semaphore()

    def place_of(offset):
        peer = lax.rem(me + offset, peers)
        return peer, {"row": peer // n_cols, "col": lax.rem(peer, n_cols)}

    for offset in range(1, peers):
        pl.semaphore_signal(barrier, inc=1, device_id=place_of(offset)[1], device_id_type=pl.DeviceIdType.MESH)
    pl.semaphore_wait(barrier, peers - 1)
    copies = []
    for offset in range(1, peers):
        peer, place = place_of(offset)
        copy = pltpu.make_async_remote_copy(
            src_ref=parts_ref.at[:, :, pl.ds(pl.multiple_of(peer * band, band), band), :],
            dst_ref=landed.at[offset - 1],
            send_sem=send_sems.at[offset - 1],
            recv_sem=recv_sems.at[offset - 1],
            device_id=place,
            device_id_type=pl.DeviceIdType.MESH,
        )
        copy.start()
        copies.append(copy)
    total = parts_ref[:, :, pl.ds(pl.multiple_of(me * band, band), band), :]
    for index, copy in enumerate(copies):
        copy.wait_recv()
        total = total + landed[index]
    out_ref[...] = total
    for copy in copies:
        copy.wait_send()


def scatter_sum(parts):
    n_rows = lax.axis_size("row")
    n_cols = lax.axis_size("col")
    peers = n_rows * n_cols
    shape = (parts.shape[0], parts.shape[1], parts.shape[2] // peers, parts.shape[3])
    return pl.pallas_call(
        functools.partial(scatter_kernel, n_rows, n_cols),
        in_specs=[pl.BlockSpec(memory_space=pltpu.VMEM)],
        out_specs=pl.BlockSpec(memory_space=pltpu.VMEM),
        out_shape=jax.ShapeDtypeStruct(shape, jnp.float32),
        scratch_shapes=[
            pltpu.VMEM((peers - 1,) + shape, jnp.float32),
            pltpu.SemaphoreType.DMA((peers - 1,)),
            pltpu.SemaphoreType.DMA((peers - 1,)),
        ],
        compiler_params=pltpu.CompilerParams(
            collective_id=0, has_side_effects=True, vmem_limit_bytes=16 * 1024 * 1024
        ),
    )(parts)


def gather_kernel(n_rows, n_cols, own_ref, cols_ref, rows_ref, local_sems, send_sems, recv_sems):
    peers = n_rows * n_cols
    deep_cols = cols_ref.shape[0]
    deep_rows = rows_ref.shape[0]
    row = lax.axis_index("row")
    col = lax.axis_index("col")
    me = row * n_cols + col
    barrier = pltpu.get_barrier_semaphore()

    def send(index, src, dst, place_row, place_col):
        copy = pltpu.make_async_remote_copy(
            src_ref=src,
            dst_ref=dst,
            send_sem=send_sems.at[index],
            recv_sem=recv_sems.at[index],
            device_id={"row": place_row, "col": place_col},
            device_id_type=pl.DeviceIdType.MESH,
        )
        copy.start()
        return copy

    steps = [(dr, dc) for dr in range(n_rows) for dc in range(n_cols) if dr or dc]
    for dr, dc in steps:
        place = {"row": lax.rem(row + dr, n_rows), "col": lax.rem(col + dc, n_cols)}
        pl.semaphore_signal(barrier, inc=1, device_id=place, device_id_type=pl.DeviceIdType.MESH)
    pl.semaphore_wait(barrier, peers - 1)
    twin = row + 1 - 2 * lax.rem(row, 2)
    keep_cols = pltpu.make_async_copy(
        own_ref.at[pl.ds(col * deep_cols, deep_cols)], cols_ref.at[:, me], local_sems.at[0]
    )
    keep_rows = pltpu.make_async_copy(
        own_ref.at[pl.ds(row * deep_rows, deep_rows)], rows_ref.at[:, me], local_sems.at[1]
    )
    keep_cols.start()
    keep_rows.start()
    first = []
    for dr, dc in steps:
        if dr % 2 == 0:
            to_row, to_col = lax.rem(row + dr, n_rows), lax.rem(col + dc, n_cols)
            src = own_ref.at[pl.ds(to_col * deep_cols, deep_cols)]
            first.append((dr, dc, send(len(first), src, cols_ref.at[:, me], to_row, to_col)))
    count = len(first)
    rest = [send(count, own_ref.at[pl.ds(col * deep_cols, deep_cols)], cols_ref.at[:, me], twin, col)]
    count += 1
    for dr, dc in steps:
        to_row, to_col = lax.rem(row + dr, n_rows), lax.rem(col + dc, n_cols)
        src = own_ref.at[pl.ds(to_row * deep_rows, deep_rows)]
        rest.append(send(count, src, rows_ref.at[:, me], to_row, to_col))
        count += 1
    for dr, dc, copy in first:
        copy.wait_recv()
        origin = lax.rem(row - dr + n_rows, n_rows) * n_cols + lax.rem(col - dc + n_cols, n_cols)
        rest.append(send(count, cols_ref.at[:, origin], cols_ref.at[:, origin], twin, col))
        count += 1
    for copy in rest:
        copy.wait_recv()
    for _, _, copy in first:
        copy.wait_send()
    for copy in rest:
        copy.wait_send()
    keep_cols.wait()
    keep_rows.wait()


def gather_sides(own):
    n_rows = lax.axis_size("row")
    n_cols = lax.axis_size("col")
    n_chan, shard_depth, width = own.shape
    peers = n_rows * n_cols
    copies = peers // 2 - 1 + 1 + peers - 1 + peers // 2 - 1
    anywhere = pl.BlockSpec(memory_space=pl.ANY)
    return pl.pallas_call(
        functools.partial(gather_kernel, n_rows, n_cols),
        in_specs=[anywhere],
        out_specs=[anywhere, anywhere],
        out_shape=[
            jax.ShapeDtypeStruct((n_chan // n_cols, peers, shard_depth, width), own.dtype),
            jax.ShapeDtypeStruct((n_chan // n_rows, peers, shard_depth, width), own.dtype),
        ],
        scratch_shapes=[
            pltpu.SemaphoreType.DMA((2,)),
            pltpu.SemaphoreType.DMA((copies,)),
            pltpu.SemaphoreType.DMA((copies,)),
        ],
        compiler_params=pltpu.CompilerParams(collective_id=1, has_side_effects=True),
    )(own)


def body(voltages, anchor_u_cells, anchor_v_cells, tile_kernel_offsets, kernel_u, kernel_v):
    samples = voltages.shape[2] // 2
    n_rows = lax.axis_size("row")
    n_cols = lax.axis_size("col")
    n_chan = lax.axis_size("chan")
    shard_depth = voltages.shape[1]
    turned = lax.all_to_all(voltages, "chan", split_axis=0, concat_axis=1, tiled=True)
    width = 2 * samples
    cols_side, rows_side = gather_sides(turned.reshape(n_chan, shard_depth, width))
    row_count = n_chan * shard_depth * n_cols
    col_count = n_chan * shard_depth * n_rows
    row_volts = rows_side.reshape(1, row_count, width)
    col_volts = cols_side.reshape(1, col_count, width)
    tile_rows = row_count // TILE_SIDE
    tile_cols = col_count // TILE_SIDE
    steps = tile_rows // STEP_ROWS
    rows = row_volts[0].reshape(steps, STEP_ROWS, TILE_SIDE, width).transpose(0, 2, 1, 3)
    rows = rows.reshape(steps, TILE_SIDE * STEP_ROWS, width)
    turned_rows = jnp.concatenate([rows[..., samples:], -rows[..., :samples]], axis=2)
    left = jnp.concatenate([rows, turned_rows], axis=1)
    cols = col_volts[0].reshape(tile_cols, TILE_SIDE, width).transpose(1, 0, 2).reshape(col_count, width)
    table_v = rolled_table(kernel_v)
    table_u = rolled_table(kernel_u)
    high_v = lax.reduce_precision(table_v, 8, 7)
    none = jnp.zeros_like(table_v)
    table = jnp.concatenate(
        [
            jnp.concatenate([high_v, none], axis=1),
            jnp.concatenate([table_v - high_v, none], axis=1),
            jnp.concatenate([none, table_u], axis=1),
        ],
        axis=0,
    ).astype(jnp.bfloat16)
    gridded = grid_tiles(
        left, cols, anchor_u_cells[0], anchor_v_cells[0], tile_kernel_offsets[0], table, 1.0 / samples
    )
    folded = gridded.reshape(1, 2, GRID_SIDE, GRID_SIDE).transpose(0, 1, 3, 2)
    return scatter_sum(folded)


def solution(mesh):
    in_specs = (
        P(None, ("chan", "row", "col"), None),
        P("chan", "row", "col"),
        P("chan", "row", "col"),
        P("chan", "row", "col"),
        P(),
        P(),
    )
    out_specs = P("chan", None, ("row", "col"), None)
    return jax.shard_map(body, mesh=mesh, in_specs=in_specs, out_specs=out_specs, check_vma=False)
```
